32 devices in a mesh: az: 8 (over z, x), rg: 4 (over y, core).
Axes of the slice: x: 2, y: 2, z: 4, core: 2. Of those that a mesh axis runs over, the one named last changes fastest.
Arguments:
- echoes: bfloat16 [2, 2048, 32768], P(None, 'rg', 'az'), may hold values from -6 to 6
- coef_table: bfloat16 [8, 5, 128, 128], replicated, may hold values from -0.3125 to 0.3125
- kern_id: int32 [256], replicated, may hold values from 0 to 7
- band_lo: int32 [256], replicated, may hold values from -2 to 2, as said below
- band_width: int32 [256], replicated, may hold values from 1 to 5
- rate: float32 [2048], P('rg'), may hold values from 4 to 40
Outputs:
- image: bfloat16 [2, 2048, 32768], P(None, ('rg', 'az'))
The draws below stay inside these ranges and needn't reach their ends.
Inputs may be any that keep to these rules, and one draw needn't show every extreme that they name: band_lo[b] + band_width[b] - 1 <= 2 for every frequency block b.
All inputs are finite; a program needn't handle non-finite values.
Results may differ from the reference program's by a relative error of at most 0.0095.
Values may be sent and summed in bfloat16 or wider, within the bound.
A program may use at most 128 MiB of HBM per device.

```python
import math
import jax
import jax.numpy as jnp
from jax import lax

A = 32768
P_SIZE = 512
Q = 64
R = 2048
TILE = 128
FB = 128
FBLK = 256
HT = 2
WMAX = 5
NKER = 8


def band_draw(key):
    blocks = lax.broadcasted_iota(jnp.int32, (FBLK,), 0)
    half = FBLK // 2
    placed = jnp.minimum(blocks, FBLK - 1 - blocks)
    growth = placed * placed * WMAX // (half * half)
    jitter = jax.random.randint(jax.random.fold_in(key, 11), (FBLK,), -1, 2)
    pinned = (placed == 0) | (placed == half - 1)
    jitter = jnp.where(pinned, 0, jitter)
    width = jnp.clip(1 + growth + jitter, 1, WMAX)
    spaces = 2 * HT + 2 - width
    picked = jax.random.randint(jax.random.fold_in(key, 12), (FBLK,), 0, 1 << 20) % spaces
    lower = picked - HT
    lower = jnp.where(blocks == 0, HT + 1 - width, lower)
    return (lower.astype(jnp.int32), width.astype(jnp.int32))


def draw_band_lo(key, part):
    return band_draw(key)[0]


def draw_band_width(key, part):
    return band_draw(key)[1]


def place_ends(values, key, smallest, high):
    dims = values.shape
    spot = [jax.random.randint(jax.random.fold_in(key, axis), (), 0, dims[axis]) for axis in range(len(dims))]
    values = values.at[tuple(spot)].set(smallest)
    longest = dims.index(max(dims))
    spot[longest] = (spot[longest] + 1) % dims[longest]
    return values.at[tuple(spot)].set(high)


def steps_of(stream_key, shape, cuts, least, high):
    gain = 1.0
    for position, blocks in cuts:
        heights = jax.random.uniform(jax.random.fold_in(jax.random.fold_in(stream_key, 6), position), (blocks,), jnp.float32, least / len(cuts), high / len(cuts))
        gain = gain * jnp.repeat(jnp.exp(heights), shape[position] // blocks).reshape((-1,) + (1,) * (len(shape) - 1 - position))
    return gain


def normal_values(key, shape, spread, bound, cuts=(), dtype=jnp.bfloat16):
    entries = jax.random.normal(key, shape, jnp.float32) * spread
    if len(cuts) > 0:
        entries = steps_of(key, shape, cuts, -0.22, 0.18) * entries
    return jnp.clip(entries, min=-bound, max=bound).astype(dtype)


def setup_inputs(seed: int = 0) -> dict:
    arg_keys = jax.random.split(jax.random.key(seed), 7)
    return {
        "echoes": normal_values(arg_keys[0], (2, R, A), 1.0, 6.0, ((1, 4), (2, 8))),
        "coef_table": normal_values(arg_keys[1], (NKER, WMAX, TILE, TILE), (3 * TILE) ** -0.5, 0.3125),
        "kern_id": place_ends(jax.random.randint(arg_keys[2], (FBLK,), 0, NKER), jax.random.fold_in(arg_keys[2], 1), 0, NKER - 1).astype(jnp.int32),
        "band_lo": draw_band_lo(jax.random.fold_in(arg_keys[6], 71), 0),
        "band_width": draw_band_width(jax.random.fold_in(arg_keys[6], 71), 0),
        "rate": jnp.clip(jnp.exp(math.log(40.0) - 2.3025851 * jax.random.uniform(arg_keys[5], (R,), jnp.float32) ** steps_of(arg_keys[5], (R,), ((0, 4),), -0.2, 0.2)), 4.0, 40.0),
    }


PRECISE = lax.Precision.HIGHEST
TWO_PI = 2.0 * math.pi

def rotation(first, second, length):
    product = lax.broadcasted_iota(jnp.int32, (first, second), 0) * lax.broadcasted_iota(jnp.int32, (first, second), 1)
    angle = (product % length).astype(jnp.float32) * (TWO_PI / length)
    return (jnp.cos(angle), jnp.sin(angle))

def tables():
    cosine_first, sine_first = rotation(P_SIZE, P_SIZE, P_SIZE)
    cosine_second, sine_second = rotation(Q, Q, Q)
    cosine_twist, sine_twist = rotation(Q, P_SIZE, A)
    scale_first = 1.0 / math.sqrt(P_SIZE)
    scale_second = 1.0 / math.sqrt(Q)
    return ((cosine_first * scale_first).astype(jnp.bfloat16), (sine_first * scale_first).astype(jnp.bfloat16), (cosine_second * scale_second).astype(jnp.bfloat16), (sine_second * scale_second).astype(jnp.bfloat16), cosine_twist, sine_twist)

def contract(form, left, right):
    return jnp.einsum(form, left.astype(jnp.float32), right.astype(jnp.float32), precision=PRECISE)

def forward(planes, factors):
    cosine_first, sine_first, cosine_second, sine_second, cosine_twist, sine_twist = factors
    width = planes.shape[1]
    grid = planes.reshape(2, width, P_SIZE, Q)
    real_part = grid[0]
    imaginary = grid[1]
    first_real = contract('cpq,pf->cqf', real_part, cosine_first) + contract('cpq,pf->cqf', imaginary, sine_first)
    first_imaginary = contract('cpq,pf->cqf', imaginary, cosine_first) - contract('cpq,pf->cqf', real_part, sine_first)
    turned_real = (first_real * cosine_twist + first_imaginary * sine_twist).astype(jnp.bfloat16)
    turned_imaginary = (first_imaginary * cosine_twist - first_real * sine_twist).astype(jnp.bfloat16)
    second_real = contract('gq,cqf->cgf', cosine_second, turned_real) + contract('gq,cqf->cgf', sine_second, turned_imaginary)
    second_imaginary = contract('gq,cqf->cgf', cosine_second, turned_imaginary) - contract('gq,cqf->cgf', sine_second, turned_real)
    return jnp.stack([second_real, second_imaginary]).reshape(2, width, A).astype(jnp.bfloat16)

def inverse(planes, factors):
    cosine_first, sine_first, cosine_second, sine_second, cosine_twist, sine_twist = factors
    width = planes.shape[1]
    grid = planes.reshape(2, width, Q, P_SIZE)
    real_part = grid[0]
    imaginary = grid[1]
    first_real = contract('qg,cgf->cqf', cosine_second, real_part) - contract('qg,cgf->cqf', sine_second, imaginary)
    first_imaginary = contract('qg,cgf->cqf', cosine_second, imaginary) + contract('qg,cgf->cqf', sine_second, real_part)
    turned_real = (first_real * cosine_twist - first_imaginary * sine_twist).astype(jnp.bfloat16)
    turned_imaginary = (first_imaginary * cosine_twist + first_real * sine_twist).astype(jnp.bfloat16)
    second_real = contract('cqf,fp->cpq', turned_real, cosine_first) - contract('cqf,fp->cpq', turned_imaginary, sine_first)
    second_imaginary = contract('cqf,fp->cpq', turned_imaginary, cosine_first) + contract('cqf,fp->cpq', turned_real, sine_first)
    return jnp.stack([second_real, second_imaginary]).reshape(2, width, A).astype(jnp.bfloat16)

def migrate(spectrum, coef_table, kern_id, band_lo, band_width, rate):
    rim = HT * TILE
    padded = jnp.pad(spectrum, ((0, 0), (rim, rim), (0, 0)))
    blocks = padded.reshape(2, R + 2 * rim, FBLK, FB).transpose(2, 0, 1, 3)
    signed = (lax.broadcasted_iota(jnp.int32, (A,), 0) + A // 2) % A - A // 2
    doppler = signed.astype(jnp.float32) / A
    squared = (doppler * doppler).reshape(FBLK, FB)

    def one_block(inputs):
        columns, lower, width, kernel_index, squared_block = inputs
        kernel = coef_table[kernel_index]
        total = jnp.zeros((2, R // TILE, TILE, FB), jnp.float32)
        for offset in range(WMAX):
            start = ((HT + lower + offset) * TILE).astype(jnp.int32)
            slab = lax.dynamic_slice_in_dim(columns, start, R, 1).reshape(2, R // TILE, TILE, FB)
            weight = jnp.where(offset < width, kernel[offset], jnp.zeros_like(kernel[offset]))
            total = total + contract('ij,ptjf->ptif', weight, slab)
        moved = total.reshape(2, R, FB)
        phase = rate[:, None] * squared_block[None, :] * TWO_PI
        cosine = jnp.cos(phase)
        sine = jnp.sin(phase)
        focused_real = moved[0] * cosine + moved[1] * sine
        focused_imaginary = moved[1] * cosine - moved[0] * sine
        return jnp.stack([focused_real, focused_imaginary]).astype(jnp.bfloat16)
    result = lax.map(one_block, (blocks, band_lo, band_width, kern_id, squared))
    return result.transpose(1, 2, 0, 3).reshape(2, R, A)

def reference(echoes, coef_table, kern_id, band_lo, band_width, rate):
    factors = tables()
    group = 256

    def forward_group(block):
        return forward(block, factors)

    def inverse_group(block):
        return inverse(block, factors)
    stacked = echoes.reshape(2, R // group, group, A).transpose(1, 0, 2, 3)
    spectrum = lax.map(forward_group, stacked).transpose(1, 0, 2, 3).reshape(2, R, A)
    focused = migrate(spectrum, coef_table, kern_id, band_lo, band_width, rate)
    stacked = focused.reshape(2, R // group, group, A).transpose(1, 0, 2, 3)
    image = lax.map(inverse_group, stacked).transpose(1, 0, 2, 3).reshape(2, R, A)
    return image
```

```python
import functools
import math

import jax
import jax.numpy as jnp
import numpy as np
import ml_dtypes
from jax import lax
from jax.experimental import pallas as pl
from jax.experimental.pallas import tpu as pltpu
from jax.sharding import PartitionSpec as P

A = 32768
HIGH = 256
LOW = 128
TILE = 128
FB = 128
HT = 2
WMAX = 5
TWO_PI = 2.0 * math.pi
VMEM = 48 * 1024 * 1024


def turn(first, second, length):
    product = np.arange(first)[:, None] * np.arange(second)[None, :]
    angle = (product % length) * (TWO_PI / length)
    return np.cos(angle), np.sin(angle)


def tables():
    c1, s1 = turn(HIGH, HIGH, HIGH)
    c1, s1 = c1 / math.sqrt(HIGH), s1 / math.sqrt(HIGH)
    c2, s2 = turn(LOW, LOW, LOW)
    c2, s2 = c2 / math.sqrt(LOW), s2 / math.sqrt(LOW)
    ct, st = turn(HIGH, LOW, A)
    bf = ml_dtypes.bfloat16
    first = np.block([[c1, s1], [-s1, c1]]).astype(bf)
    second = np.block([[c2, s2], [-s2, c2]]).astype(bf)
    second_back = np.block([[c2, -s2], [s2, c2]]).astype(bf)
    first_back = np.block([[c1, -s1], [s1, c1]]).astype(bf)
    ct, st = ct.astype(np.float32), st.astype(np.float32)
    return first, second, ct, st, second_back, first_back, ct.T.copy(), st.T.copy()


def circle():
    nodes = 0.5 * np.cos(np.pi * (np.arange(400) + 0.5) / 400)
    u = nodes * nodes
    sine = np.polynomial.Polynomial.fit(u, np.sin(TWO_PI * nodes) / nodes, 7, domain=[0, 0.25])
    cosine = np.polynomial.Polynomial.fit(u, np.cos(TWO_PI * nodes), 7, domain=[0, 0.25])
    return (
        [float(v) for v in sine.convert().coef],
        [float(v) for v in cosine.convert().coef],
    )


def horner(coefs, u):
    total = jnp.full_like(u, coefs[-1])
    for value in coefs[-2::-1]:
        total = total * u + value
    return total


def dot(left, right):
    return jnp.dot(left, right, preferred_element_type=jnp.float32)


def dot_t(left, right):
    return lax.dot_general(left, right, (((1,), (1,)), ((), ())), preferred_element_type=jnp.float32)


def forward_kernel(x_ref, first_ref, second_ref, ct_ref, st_ref, o_ref, held):
    rows = x_ref.shape[2]
    members, _, per, _, _ = o_ref.shape

    def pair(index, carry):
        both = []
        for j in range(2):
            r = index * 2 + j
            both.append(
                jnp.concatenate(
                    [x_ref[:, p, r].reshape(HIGH, LOW) for p in range(2)], axis=0
                )
            )
        y = dot(first_ref[...], jnp.concatenate(both, axis=1))
        for j in range(2):
            yr = y[:HIGH, j * LOW : (j + 1) * LOW]
            yi = y[HIGH:, j * LOW : (j + 1) * LOW]
            ct, st = ct_ref[...], st_ref[...]
            turned = jnp.concatenate(
                [
                    (yr * ct + yi * st).astype(jnp.bfloat16),
                    (yi * ct - yr * st).astype(jnp.bfloat16),
                ],
                axis=1,
            )
            held[index * 2 + j] = dot_t(second_ref[...], turned)
        return carry

    lax.fori_loop(0, rows // 2, pair, 0)
    for p in range(2):
        for d in range(members):
            lo = p * LOW + d * per
            piece = jnp.swapaxes(held[:, lo : lo + per, :], 0, 1)
            o_ref[d, p] = piece.astype(jnp.bfloat16)


def inverse_kernel(x_ref, second_ref, first_ref, ct_ref, st_ref, o_ref, held):
    members, _, per, rows, _ = x_ref.shape
    group = max(1, 16 // per)
    for p in range(2):
        for s in range(0, members, group):
            pieces = [
                jnp.swapaxes(x_ref[s + g, p].astype(jnp.float32), 0, 1) for g in range(group)
            ]
            piece = pieces[0] if group == 1 else jnp.concatenate(pieces, axis=1)
            lo = p * LOW + s * per
            held[:, lo : lo + group * per, :] = piece.astype(jnp.bfloat16)

    def pair(index, carry):
        both = []
        for j in range(2):
            u = dot(second_ref[...], held[index * 2 + j])
            ur, ui = u[:LOW], u[LOW:]
            ct, st = ct_ref[...], st_ref[...]
            both.append(
                jnp.concatenate(
                    [
                        (ur * ct - ui * st).astype(jnp.bfloat16),
                        (ui * ct + ur * st).astype(jnp.bfloat16),
                    ],
                    axis=1,
                )
            )
        out = dot_t(first_ref[...], jnp.concatenate(both, axis=0)).astype(jnp.bfloat16)
        for p in range(2):
            for j in range(2):
                o_ref[p, index * 2 + j] = out[p * HIGH : (p + 1) * HIGH, j * LOW : (j + 1) * LOW]
        return carry

    lax.fori_loop(0, rows // 2, pair, 0)


def migrate_kernel(
    place, kern_id, band_lo, band_width, low_ref, mid_ref, high_ref, coef_ref, rate_ref, o_ref, held
):
    sine_coefs, cosine_coefs = circle()
    step = pl.program_id(0)
    columns = mid_ref.shape[3]
    range_rows = mid_ref.shape[0] * columns
    rim = HT * TILE
    full = range_rows + 2 * rim
    halves = HIGH // FB

    @pl.when(step == 0)
    def _():
        held[full:, :] = jnp.zeros((held.shape[0] - full, held.shape[1]), held.dtype)

    row = 0
    for ref in (low_ref, mid_ref, high_ref):
        for s in range(ref.shape[0]):
            for p in range(2):
                for h in range(halves):
                    lane = (h * 2 + p) * FB
                    held[row : row + columns, lane : lane + FB] = ref[
                        s, p, 0, :, h * FB : (h + 1) * FB
                    ]
            row += columns

    for h in range(halves):
        block = place[0] + step * halves + h
        lower = band_lo[block]
        width = band_width[block]
        kernel = kern_id[block]
        weights = jnp.concatenate(
            [
                jnp.where(
                    k < width, coef_ref[kernel, k].astype(jnp.float32), 0.0
                ).astype(jnp.bfloat16)
                for k in range(WMAX)
            ],
            axis=1,
        )
        lanes = lax.broadcasted_iota(jnp.int32, (1, FB), 1)
        signed = (block * FB + lanes + A // 2) % A - A // 2
        doppler = signed.astype(jnp.float32) * (1.0 / A)
        squared = doppler * doppler
        for t in range(range_rows // TILE):
            start = pl.multiple_of((t + HT + lower) * TILE, TILE)
            moved = dot(
                weights, held[pl.ds(start, WMAX * TILE), h * 2 * FB : (h + 1) * 2 * FB]
            )
            turns = rate_ref[t * TILE : (t + 1) * TILE, :] * squared
            x = turns - jnp.round(turns)
            u = x * x
            sine = horner(sine_coefs, u) * x
            cosine = horner(cosine_coefs, u)
            mr, mi = moved[:, :FB], moved[:, FB:]
            done = (
                (mr * cosine + mi * sine).astype(jnp.bfloat16),
                (mi * cosine - mr * sine).astype(jnp.bfloat16),
            )
            for p in range(2):
                for part in range(TILE // columns):
                    o_ref[t * (TILE // columns) + part, p, 0, :, h * FB : (h + 1) * FB] = done[p][
                        part * columns : (part + 1) * columns
                    ]


def whole_spec(shape):
    return pl.BlockSpec(shape, lambda *_: (0,) * len(shape))


def params():
    return pltpu.CompilerParams(vmem_limit_bytes=VMEM)


def forward(x, first, second, ct, st):
    members, _, columns, fold, _ = x.shape
    per = LOW // members
    rows = min(16, columns)
    return pl.pallas_call(
        forward_kernel,
        grid=(columns // rows,),
        in_specs=[
            pl.BlockSpec((members, 2, rows, fold, LOW), lambda i: (0, 0, i, 0, 0)),
            whole_spec(first.shape),
            whole_spec(second.shape),
            whole_spec(ct.shape),
            whole_spec(st.shape),
        ],
        out_specs=pl.BlockSpec((members, 2, per, rows, HIGH), lambda i: (0, 0, 0, i, 0)),
        out_shape=jax.ShapeDtypeStruct((members, 2, per, columns, HIGH), jnp.bfloat16),
        scratch_shapes=[pltpu.VMEM((rows, 2 * LOW, HIGH), jnp.float32)],
        compiler_params=params(),
    )(x, first, second, ct, st)


def inverse(x, second, first, ct, st):
    members, _, per, columns, _ = x.shape
    rows = min(16, columns)
    return pl.pallas_call(
        inverse_kernel,
        grid=(columns // rows,),
        in_specs=[
            pl.BlockSpec((members, 2, per, rows, HIGH), lambda i: (0, 0, 0, i, 0)),
            whole_spec(second.shape),
            whole_spec(first.shape),
            whole_spec(ct.shape),
            whole_spec(st.shape),
        ],
        out_specs=pl.BlockSpec((2, rows, HIGH, LOW), lambda i: (0, i, 0, 0)),
        out_shape=jax.ShapeDtypeStruct((2, columns, HIGH, LOW), jnp.bfloat16),
        scratch_shapes=[pltpu.VMEM((rows, 2 * LOW, HIGH), jnp.bfloat16)],
        compiler_params=params(),
    )(x, second, first, ct, st)


def migrate(place, kern_id, band_lo, band_width, low, mid, high, coef, rate):
    members, _, per, columns, _ = mid.shape
    range_rows = members * columns
    depth = range_rows + (2 * HT + WMAX - 1) * TILE

    def chunk(count):
        return pl.BlockSpec((count, 2, 1, columns, HIGH), lambda i, *_: (0, 0, i, 0, 0))

    return pl.pallas_call(
        migrate_kernel,
        grid_spec=pltpu.PrefetchScalarGridSpec(
            num_scalar_prefetch=4,
            grid=(per,),
            in_specs=[
                chunk(low.shape[0]),
                chunk(members),
                chunk(high.shape[0]),
                whole_spec(coef.shape),
                whole_spec((range_rows, 1)),
            ],
            out_specs=chunk(members),
            scratch_shapes=[pltpu.VMEM((depth, 2 * HIGH), jnp.bfloat16)],
        ),
        out_shape=jax.ShapeDtypeStruct(mid.shape, jnp.bfloat16),
        compiler_params=params(),
    )(place, kern_id, band_lo, band_width, low, mid, high, coef, rate.reshape(-1, 1))


def exchange(block):
    return lax.all_to_all(block, "az", split_axis=0, concat_axis=0, tiled=True)


def body(echoes, coef_table, kern_id, band_lo, band_width, rate):
    first, second, ct, st, second_back, first_back, ct_back, st_back = map(jnp.asarray, tables())
    members = lax.axis_size("az")
    here = lax.axis_index("az")
    range_rows, lines = echoes.shape[1:]
    columns = range_rows // members
    per = LOW // members
    grouped = echoes.reshape(2, members, columns, lines // LOW, LOW).transpose(1, 0, 2, 3, 4)
    spectrum = exchange(forward(exchange(grouped), first, second, ct, st))
    chunks = HT * TILE // columns
    count = lax.axis_size("rg")
    up = [(i, i + 1) for i in range(count - 1)]
    down = [(i + 1, i) for i in range(count - 1)]
    low = lax.ppermute(spectrum[members - chunks :], "rg", up)
    high = lax.ppermute(spectrum[:chunks], "rg", down)
    place = (here * per * (HIGH // FB)).astype(jnp.int32).reshape(1)
    focused = migrate(
        place, kern_id, band_lo, band_width, low, spectrum, high, coef_table, rate
    )
    image = inverse(exchange(focused), second_back, first_back, ct_back, st_back)
    return image.reshape(2, columns, A)


def solution(mesh):
    in_specs = (P(None, "rg", "az"), P(), P(), P(), P(), P("rg"))
    out_specs = P(None, ("rg", "az"), None)
    return jax.shard_map(body, mesh=mesh, in_specs=in_specs, out_specs=out_specs, check_vma=False)
```

```python
import functools
import math

import jax
import jax.numpy as jnp
import numpy as np
import ml_dtypes
from jax import lax
from jax.experimental import pallas as pl
from jax.experimental.pallas import tpu as pltpu
from jax.sharding import PartitionSpec as P

A = 32768
HIGH = 256
LOW = 128
TILE = 128
FB = 128
HT = 2
WMAX = 5
TWO_PI = 2.0 * math.pi
VMEM = 48 * 1024 * 1024


def turn(first, second, length):
    product = np.arange(first)[:, None] * np.arange(second)[None, :]
    angle = (product % length) * (TWO_PI / length)
    return np.cos(angle), np.sin(angle)


def tables():
    c1, s1 = turn(HIGH, HIGH, HIGH)
    c1, s1 = c1 / math.sqrt(HIGH), s1 / math.sqrt(HIGH)
    c2, s2 = turn(LOW, LOW, LOW)
    c2, s2 = c2 / math.sqrt(LOW), s2 / math.sqrt(LOW)
    ct, st = turn(HIGH, LOW, A)
    bf = ml_dtypes.bfloat16
    first = np.block([[c1, s1], [-s1, c1]]).astype(bf)
    second = np.block([[c2, s2], [-s2, c2]]).astype(bf)
    second_back = np.block([[c2, -s2], [s2, c2]]).astype(bf)
    first_back = np.block([[c1, -s1], [s1, c1]]).astype(bf)
    ct, st = ct.astype(np.float32), st.astype(np.float32)
    return first, second, ct, st, second_back, first_back, ct.T.copy(), st.T.copy()


def circle():
    nodes = 0.5 * np.cos(np.pi * (np.arange(400) + 0.5) / 400)
    u = nodes * nodes
    sine = np.polynomial.Polynomial.fit(u, np.sin(TWO_PI * nodes) / nodes, 7, domain=[0, 0.25])
    cosine = np.polynomial.Polynomial.fit(u, np.cos(TWO_PI * nodes), 7, domain=[0, 0.25])
    return (
        [float(v) for v in sine.convert().coef],
        [float(v) for v in cosine.convert().coef],
    )


def horner(coefs, u):
    total = jnp.full_like(u, coefs[-1])
    for value in coefs[-2::-1]:
        total = total * u + value
    return total


def dot(left, right):
    return jnp.dot(left, right, preferred_element_type=jnp.float32)


def dot_t(left, right):
    return lax.dot_general(left, right, (((1,), (1,)), ((), ())), preferred_element_type=jnp.float32)


def forward_kernel(x_ref, first_ref, second_ref, ct_ref, st_ref, o_ref, held, lines):
    rows = x_ref.shape[2]
    members, _, per, _, _ = o_ref.shape
    fold = x_ref.shape[3] // LOW
    for p in range(2):
        for s in range(members):
            tall = jnp.stack(
                [
                    x_ref[s, p, :, a * LOW : (a + 1) * LOW].astype(jnp.float32)
                    for a in range(fold)
                ]
            )
            lo = p * HIGH + s * fold
            lines[:, lo : lo + fold, :] = jnp.swapaxes(tall, 0, 1)

    def pair(index, carry):
        both = []
        for j in range(2):
            r = index * 2 + j
            both.append(lines[r].astype(jnp.bfloat16))
        y = dot(first_ref[...], jnp.concatenate(both, axis=1))
        for j in range(2):
            yr = y[:HIGH, j * LOW : (j + 1) * LOW]
            yi = y[HIGH:, j * LOW : (j + 1) * LOW]
            ct, st = ct_ref[...], st_ref[...]
            turned = jnp.concatenate(
                [
                    (yr * ct + yi * st).astype(jnp.bfloat16),
                    (yi * ct - yr * st).astype(jnp.bfloat16),
                ],
                axis=1,
            )
            held[index * 2 + j] = dot_t(second_ref[...], turned)
        return carry

    lax.fori_loop(0, rows // 2, pair, 0)
    for p in range(2):
        for d in range(members):
            lo = p * LOW + d * per
            piece = jnp.swapaxes(held[:, lo : lo + per, :], 0, 1)
            o_ref[d, p] = piece.astype(jnp.bfloat16)


def inverse_kernel(x_ref, second_ref, first_ref, ct_ref, st_ref, o_ref, held, lines):
    members, _, per, rows, _ = x_ref.shape
    group = max(1, 16 // per)
    for p in range(2):
        for s in range(0, members, group):
            pieces = [
                jnp.swapaxes(x_ref[s + g, p].astype(jnp.float32), 0, 1) for g in range(group)
            ]
            piece = pieces[0] if group == 1 else jnp.concatenate(pieces, axis=1)
            lo = p * LOW + s * per
            held[:, lo : lo + group * per, :] = piece.astype(jnp.bfloat16)

    def pair(index, carry):
        both = []
        for j in range(2):
            u = dot(second_ref[...], held[index * 2 + j])
            ur, ui = u[:LOW], u[LOW:]
            ct, st = ct_ref[...], st_ref[...]
            both.append(
                jnp.concatenate(
                    [
                        (ur * ct - ui * st).astype(jnp.bfloat16),
                        (ui * ct + ur * st).astype(jnp.bfloat16),
                    ],
                    axis=1,
                )
            )
        out = dot_t(first_ref[...], jnp.concatenate(both, axis=0))
        for j in range(2):
            lines[index * 2 + j] = out[:, j * LOW : (j + 1) * LOW]
        return carry

    lax.fori_loop(0, rows // 2, pair, 0)
    for p in range(2):
        for a in range(0, HIGH, 16):
            lo = p * HIGH + a
            wide = jnp.swapaxes(lines[:, lo : lo + 16, :], 0, 1).astype(jnp.bfloat16)
            for b in range(16):
                o_ref[p, :, (a + b) * LOW : (a + b + 1) * LOW] = wide[b]


def migrate_kernel(
    place, kern_id, band_lo, band_width, low_ref, mid_ref, high_ref, coef_ref, rate_ref, o_ref, held
):
    sine_coefs, cosine_coefs = circle()
    step = pl.program_id(0)
    columns = mid_ref.shape[3]
    range_rows = mid_ref.shape[0] * columns
    rim = HT * TILE
    full = range_rows + 2 * rim
    halves = HIGH // FB

    @pl.when(step == 0)
    def _():
        held[full:, :] = jnp.zeros((held.shape[0] - full, held.shape[1]), held.dtype)

    row = 0
    for ref in (low_ref, mid_ref, high_ref):
        for s in range(ref.shape[0]):
            for p in range(2):
                for h in range(halves):
                    lane = (h * 2 + p) * FB
                    held[row : row + columns, lane : lane + FB] = ref[
                        s, p, 0, :, h * FB : (h + 1) * FB
                    ]
            row += columns

    for h in range(halves):
        block = place[0] + step * halves + h
        lower = band_lo[block]
        width = band_width[block]
        kernel = kern_id[block]
        weights = jnp.concatenate(
            [
                jnp.where(
                    k < width, coef_ref[kernel, k].astype(jnp.float32), 0.0
                ).astype(jnp.bfloat16)
                for k in range(WMAX)
            ],
            axis=1,
        )
        lanes = lax.broadcasted_iota(jnp.int32, (1, FB), 1)
        signed = (block * FB + lanes + A // 2) % A - A // 2
        doppler = signed.astype(jnp.float32) * (1.0 / A)
        squared = doppler * doppler
        for t in range(range_rows // TILE):
            start = pl.multiple_of((t + HT + lower) * TILE, TILE)
            moved = dot(
                weights, held[pl.ds(start, WMAX * TILE), h * 2 * FB : (h + 1) * 2 * FB]
            )
            turns = rate_ref[t * TILE : (t + 1) * TILE, :] * squared
            x = turns - jnp.round(turns)
            u = x * x
            sine = horner(sine_coefs, u) * x
            cosine = horner(cosine_coefs, u)
            mr, mi = moved[:, :FB], moved[:, FB:]
            done = (
                (mr * cosine + mi * sine).astype(jnp.bfloat16),
                (mi * cosine - mr * sine).astype(jnp.bfloat16),
            )
            for p in range(2):
                for part in range(TILE // columns):
                    o_ref[t * (TILE // columns) + part, p, 0, :, h * FB : (h + 1) * FB] = done[p][
                        part * columns : (part + 1) * columns
                    ]


def whole_spec(shape):
    return pl.BlockSpec(shape, lambda *_: (0,) * len(shape))


def params():
    return pltpu.CompilerParams(vmem_limit_bytes=VMEM)


def forward(x, first, second, ct, st):
    members, _, columns, length = x.shape
    per = LOW // members
    rows = min(16, columns)
    return pl.pallas_call(
        forward_kernel,
        grid=(columns // rows,),
        in_specs=[
            pl.BlockSpec((members, 2, rows, length), lambda i: (0, 0, i, 0)),
            whole_spec(first.shape),
            whole_spec(second.shape),
            whole_spec(ct.shape),
            whole_spec(st.shape),
        ],
        out_specs=pl.BlockSpec((members, 2, per, rows, HIGH), lambda i: (0, 0, 0, i, 0)),
        out_shape=jax.ShapeDtypeStruct((members, 2, per, columns, HIGH), jnp.bfloat16),
        scratch_shapes=[
            pltpu.VMEM((rows, 2 * LOW, HIGH), jnp.float32),
            pltpu.VMEM((rows, 2 * HIGH, LOW), jnp.float32),
        ],
        compiler_params=params(),
    )(x, first, second, ct, st)


def inverse(x, second, first, ct, st):
    members, _, per, columns, _ = x.shape
    rows = min(16, columns)
    return pl.pallas_call(
        inverse_kernel,
        grid=(columns // rows,),
        in_specs=[
            pl.BlockSpec((members, 2, per, rows, HIGH), lambda i: (0, 0, 0, i, 0)),
            whole_spec(second.shape),
            whole_spec(first.shape),
            whole_spec(ct.shape),
            whole_spec(st.shape),
        ],
        out_specs=pl.BlockSpec((2, rows, A), lambda i: (0, i, 0)),
        out_shape=jax.ShapeDtypeStruct((2, columns, A), jnp.bfloat16),
        scratch_shapes=[
            pltpu.VMEM((rows, 2 * LOW, HIGH), jnp.bfloat16),
            pltpu.VMEM((rows, 2 * HIGH, LOW), jnp.float32),
        ],
        compiler_params=params(),
    )(x, second, first, ct, st)


def migrate(place, kern_id, band_lo, band_width, low, mid, high, coef, rate):
    members, _, per, columns, _ = mid.shape
    range_rows = members * columns
    depth = range_rows + (2 * HT + WMAX - 1) * TILE

    def chunk(count):
        return pl.BlockSpec((count, 2, 1, columns, HIGH), lambda i, *_: (0, 0, i, 0, 0))

    return pl.pallas_call(
        migrate_kernel,
        grid_spec=pltpu.PrefetchScalarGridSpec(
            num_scalar_prefetch=4,
            grid=(per,),
            in_specs=[
                chunk(low.shape[0]),
                chunk(members),
                chunk(high.shape[0]),
                whole_spec(coef.shape),
                whole_spec((range_rows, 1)),
            ],
            out_specs=chunk(members),
            scratch_shapes=[pltpu.VMEM((depth, 2 * HIGH), jnp.bfloat16)],
        ),
        out_shape=jax.ShapeDtypeStruct(mid.shape, jnp.bfloat16),
        compiler_params=params(),
    )(place, kern_id, band_lo, band_width, low, mid, high, coef, rate.reshape(-1, 1))


def exchange(block):
    return lax.all_to_all(block, "az", split_axis=0, concat_axis=0, tiled=True)


def body(echoes, coef_table, kern_id, band_lo, band_width, rate):
    first, second, ct, st, second_back, first_back, ct_back, st_back = map(jnp.asarray, tables())
    members = lax.axis_size("az")
    here = lax.axis_index("az")
    range_rows, lines = echoes.shape[1:]
    columns = range_rows // members
    per = LOW // members
    grouped = echoes.reshape(2, members, columns, lines).transpose(1, 0, 2, 3)
    spectrum = exchange(forward(exchange(grouped), first, second, ct, st))
    chunks = HT * TILE // columns
    count = lax.axis_size("rg")
    up = [(i, i + 1) for i in range(count - 1)]
    down = [(i + 1, i) for i in range(count - 1)]
    low = lax.ppermute(spectrum[members - chunks :], "rg", up)
    high = lax.ppermute(spectrum[:chunks], "rg", down)
    place = (here * per * (HIGH // FB)).astype(jnp.int32).reshape(1)
    focused = migrate(
        place, kern_id, band_lo, band_width, low, spectrum, high, coef_table, rate
    )
    image = inverse(exchange(focused), second_back, first_back, ct_back, st_back)
    return image


def solution(mesh):
    in_specs = (P(None, "rg", "az"), P(), P(), P(), P(), P("rg"))
    out_specs = P(None, ("rg", "az"), None)
    return jax.shard_map(body, mesh=mesh, in_specs=in_specs, out_specs=out_specs, check_vma=False)
```

```python
import functools
import math

import jax
import jax.numpy as jnp
import numpy as np
import ml_dtypes
from jax import lax
from jax.experimental import pallas as pl
from jax.experimental.pallas import tpu as pltpu
from jax.sharding import PartitionSpec as P

A = 32768
HIGH = 256
LOW = 128
TILE = 128
FB = 128
HT = 2
WMAX = 5
TWO_PI = 2.0 * math.pi
VMEM = 48 * 1024 * 1024


def turn(first, second, length):
    product = np.arange(first)[:, None] * np.arange(second)[None, :]
    angle = (product % length) * (TWO_PI / length)
    return np.cos(angle), np.sin(angle)


def tables():
    c1, s1 = turn(HIGH, HIGH, HIGH)
    c1, s1 = c1 / math.sqrt(HIGH), s1 / math.sqrt(HIGH)
    c2, s2 = turn(LOW, LOW, LOW)
    c2, s2 = c2 / math.sqrt(LOW), s2 / math.sqrt(LOW)
    ct, st = turn(HIGH, LOW, A)
    bf = ml_dtypes.bfloat16
    first = np.block([[c1, s1], [-s1, c1]]).astype(bf)
    second = np.block([[c2, s2], [-s2, c2]]).astype(bf)
    second_back = np.block([[c2, -s2], [s2, c2]]).astype(bf)
    first_back = np.block([[c1, -s1], [s1, c1]]).astype(bf)
    ct, st = ct.astype(np.float32), st.astype(np.float32)
    return first, second, ct, st, second_back, first_back, ct.T.copy(), st.T.copy()


def circle():
    nodes = 0.5 * np.cos(np.pi * (np.arange(400) + 0.5) / 400)
    u = nodes * nodes
    sine = np.polynomial.Polynomial.fit(u, np.sin(TWO_PI * nodes) / nodes, 7, domain=[0, 0.25])
    cosine = np.polynomial.Polynomial.fit(u, np.cos(TWO_PI * nodes), 7, domain=[0, 0.25])
    return (
        [float(v) for v in sine.convert().coef],
        [float(v) for v in cosine.convert().coef],
    )


def horner(coefs, u):
    total = jnp.full_like(u, coefs[-1])
    for value in coefs[-2::-1]:
        total = total * u + value
    return total


def dot(left, right):
    return jnp.dot(left, right, preferred_element_type=jnp.float32)


def dot_t(left, right):
    return lax.dot_general(left, right, (((1,), (1,)), ((), ())), preferred_element_type=jnp.float32)


def forward_kernel(real_ref, imaginary_ref, first_ref, second_ref, ct_ref, st_ref, o_ref, held, lines):
    planes = (real_ref, imaginary_ref)
    rows = real_ref.shape[1]
    members, _, per, _, _ = o_ref.shape
    fold = real_ref.shape[2] // LOW
    for p in range(2):
        for s in range(members):
            tall = jnp.stack(
                [
                    planes[p][s, :, a * LOW : (a + 1) * LOW].astype(jnp.float32)
                    for a in range(fold)
                ]
            )
            lo = p * HIGH + s * fold
            lines[:, lo : lo + fold, :] = jnp.swapaxes(tall, 0, 1)

    def pair(index, carry):
        both = []
        for j in range(2):
            r = index * 2 + j
            both.append(lines[r].astype(jnp.bfloat16))
        y = dot(first_ref[...], jnp.concatenate(both, axis=1))
        for j in range(2):
            yr = y[:HIGH, j * LOW : (j + 1) * LOW]
            yi = y[HIGH:, j * LOW : (j + 1) * LOW]
            ct, st = ct_ref[...], st_ref[...]
            turned = jnp.concatenate(
                [
                    (yr * ct + yi * st).astype(jnp.bfloat16),
                    (yi * ct - yr * st).astype(jnp.bfloat16),
                ],
                axis=1,
            )
            held[index * 2 + j] = dot_t(second_ref[...], turned)
        return carry

    lax.fori_loop(0, rows // 2, pair, 0)
    for p in range(2):
        for d in range(members):
            lo = p * LOW + d * per
            piece = jnp.swapaxes(held[:, lo : lo + per, :], 0, 1)
            o_ref[d, p] = piece.astype(jnp.bfloat16)


def inverse_kernel(x_ref, second_ref, first_ref, ct_ref, st_ref, o_ref, held, lines):
    members, _, per, rows, _ = x_ref.shape
    group = max(1, 16 // per)
    for p in range(2):
        for s in range(0, members, group):
            pieces = [
                jnp.swapaxes(x_ref[s + g, p].astype(jnp.float32), 0, 1) for g in range(group)
            ]
            piece = pieces[0] if group == 1 else jnp.concatenate(pieces, axis=1)
            lo = p * LOW + s * per
            held[:, lo : lo + group * per, :] = piece.astype(jnp.bfloat16)

    def pair(index, carry):
        both = []
        for j in range(2):
            u = dot(second_ref[...], held[index * 2 + j])
            ur, ui = u[:LOW], u[LOW:]
            ct, st = ct_ref[...], st_ref[...]
            both.append(
                jnp.concatenate(
                    [
                        (ur * ct - ui * st).astype(jnp.bfloat16),
                        (ui * ct + ur * st).astype(jnp.bfloat16),
                    ],
                    axis=1,
                )
            )
        out = dot_t(first_ref[...], jnp.concatenate(both, axis=0))
        for j in range(2):
            lines[index * 2 + j] = out[:, j * LOW : (j + 1) * LOW]
        return carry

    lax.fori_loop(0, rows // 2, pair, 0)
    for p in range(2):
        for a in range(0, HIGH, 16):
            lo = p * HIGH + a
            wide = jnp.swapaxes(lines[:, lo : lo + 16, :], 0, 1).astype(jnp.bfloat16)
            for b in range(16):
                o_ref[p, :, (a + b) * LOW : (a + b + 1) * LOW] = wide[b]


def migrate_kernel(
    place, kern_id, band_lo, band_width, low_ref, mid_ref, high_ref, coef_ref, rate_ref, o_ref, held
):
    sine_coefs, cosine_coefs = circle()
    step = pl.program_id(0)
    columns = mid_ref.shape[3]
    range_rows = mid_ref.shape[0] * columns
    rim = HT * TILE
    full = range_rows + 2 * rim
    halves = HIGH // FB

    @pl.when(step == 0)
    def _():
        held[full:, :] = jnp.zeros((held.shape[0] - full, held.shape[1]), held.dtype)

    row = 0
    for ref in (low_ref, mid_ref, high_ref):
        for s in range(ref.shape[0]):
            for p in range(2):
                for h in range(halves):
                    lane = (h * 2 + p) * FB
                    held[row : row + columns, lane : lane + FB] = ref[
                        s, p, 0, :, h * FB : (h + 1) * FB
                    ]
            row += columns

    for h in range(halves):
        block = place[0] + step * halves + h
        lower = band_lo[block]
        width = band_width[block]
        kernel = kern_id[block]
        weights = jnp.concatenate(
            [
                jnp.where(
                    k < width, coef_ref[kernel, k].astype(jnp.float32), 0.0
                ).astype(jnp.bfloat16)
                for k in range(WMAX)
            ],
            axis=1,
        )
        lanes = lax.broadcasted_iota(jnp.int32, (1, FB), 1)
        signed = (block * FB + lanes + A // 2) % A - A // 2
        doppler = signed.astype(jnp.float32) * (1.0 / A)
        squared = doppler * doppler
        for t in range(range_rows // TILE):
            start = pl.multiple_of((t + HT + lower) * TILE, TILE)
            moved = dot(
                weights, held[pl.ds(start, WMAX * TILE), h * 2 * FB : (h + 1) * 2 * FB]
            )
            turns = rate_ref[t * TILE : (t + 1) * TILE, :] * squared
            x = turns - jnp.round(turns)
            u = x * x
            sine = horner(sine_coefs, u) * x
            cosine = horner(cosine_coefs, u)
            mr, mi = moved[:, :FB], moved[:, FB:]
            done = (
                (mr * cosine + mi * sine).astype(jnp.bfloat16),
                (mi * cosine - mr * sine).astype(jnp.bfloat16),
            )
            for p in range(2):
                for part in range(TILE // columns):
                    o_ref[t * (TILE // columns) + part, p, 0, :, h * FB : (h + 1) * FB] = done[p][
                        part * columns : (part + 1) * columns
                    ]


def whole_spec(shape):
    return pl.BlockSpec(shape, lambda *_: (0,) * len(shape))


def params():
    return pltpu.CompilerParams(vmem_limit_bytes=VMEM)


def forward(real, imaginary, first, second, ct, st):
    members, columns, length = real.shape
    per = LOW // members
    rows = min(16, columns)
    return pl.pallas_call(
        forward_kernel,
        grid=(columns // rows,),
        in_specs=[
            pl.BlockSpec((members, rows, length), lambda i: (0, i, 0)),
            pl.BlockSpec((members, rows, length), lambda i: (0, i, 0)),
            whole_spec(first.shape),
            whole_spec(second.shape),
            whole_spec(ct.shape),
            whole_spec(st.shape),
        ],
        out_specs=pl.BlockSpec((members, 2, per, rows, HIGH), lambda i: (0, 0, 0, i, 0)),
        out_shape=jax.ShapeDtypeStruct((members, 2, per, columns, HIGH), jnp.bfloat16),
        scratch_shapes=[
            pltpu.VMEM((rows, 2 * LOW, HIGH), jnp.float32),
            pltpu.VMEM((rows, 2 * HIGH, LOW), jnp.float32),
        ],
        compiler_params=params(),
    )(real, imaginary, first, second, ct, st)


def inverse(x, second, first, ct, st):
    members, _, per, columns, _ = x.shape
    rows = min(16, columns)
    return pl.pallas_call(
        inverse_kernel,
        grid=(columns // rows,),
        in_specs=[
            pl.BlockSpec((members, 2, per, rows, HIGH), lambda i: (0, 0, 0, i, 0)),
            whole_spec(second.shape),
            whole_spec(first.shape),
            whole_spec(ct.shape),
            whole_spec(st.shape),
        ],
        out_specs=pl.BlockSpec((2, rows, A), lambda i: (0, i, 0)),
        out_shape=jax.ShapeDtypeStruct((2, columns, A), jnp.bfloat16),
        scratch_shapes=[
            pltpu.VMEM((rows, 2 * LOW, HIGH), jnp.bfloat16),
            pltpu.VMEM((rows, 2 * HIGH, LOW), jnp.float32),
        ],
        compiler_params=params(),
    )(x, second, first, ct, st)


def migrate(place, kern_id, band_lo, band_width, low, mid, high, coef, rate):
    members, _, per, columns, _ = mid.shape
    range_rows = members * columns
    depth = range_rows + (2 * HT + WMAX - 1) * TILE

    def chunk(count):
        return pl.BlockSpec((count, 2, 1, columns, HIGH), lambda i, *_: (0, 0, i, 0, 0))

    return pl.pallas_call(
        migrate_kernel,
        grid_spec=pltpu.PrefetchScalarGridSpec(
            num_scalar_prefetch=4,
            grid=(per,),
            in_specs=[
                chunk(low.shape[0]),
                chunk(members),
                chunk(high.shape[0]),
                whole_spec(coef.shape),
                whole_spec((range_rows, 1)),
            ],
            out_specs=chunk(members),
            scratch_shapes=[pltpu.VMEM((depth, 2 * HIGH), jnp.bfloat16)],
        ),
        out_shape=jax.ShapeDtypeStruct(mid.shape, jnp.bfloat16),
        compiler_params=params(),
    )(place, kern_id, band_lo, band_width, low, mid, high, coef, rate.reshape(-1, 1))


def exchange(block):
    return lax.all_to_all(block, "az", split_axis=0, concat_axis=0, tiled=True)


def body(echoes, coef_table, kern_id, band_lo, band_width, rate):
    first, second, ct, st, second_back, first_back, ct_back, st_back = map(jnp.asarray, tables())
    members = lax.axis_size("az")
    here = lax.axis_index("az")
    range_rows, lines = echoes.shape[1:]
    columns = range_rows // members
    per = LOW // members
    grouped = echoes.reshape(2, members, columns, lines)
    spectrum = exchange(forward(exchange(grouped[0]), exchange(grouped[1]), first, second, ct, st))
    chunks = HT * TILE // columns
    count = lax.axis_size("rg")
    up = [(i, i + 1) for i in range(count - 1)]
    down = [(i + 1, i) for i in range(count - 1)]
    low = lax.ppermute(spectrum[members - chunks :], "rg", up)
    high = lax.ppermute(spectrum[:chunks], "rg", down)
    place = (here * per * (HIGH // FB)).astype(jnp.int32).reshape(1)
    focused = migrate(
        place, kern_id, band_lo, band_width, low, spectrum, high, coef_table, rate
    )
    image = inverse(exchange(focused), second_back, first_back, ct_back, st_back)
    return image


def solution(mesh):
    in_specs = (P(None, "rg", "az"), P(), P(), P(), P(), P("rg"))
    out_specs = P(None, ("rg", "az"), None)
    return jax.shard_map(body, mesh=mesh, in_specs=in_specs, out_specs=out_specs, check_vma=False)
```
